256 devices in a mesh: row: 4 (over x_hi, core), col: 16 (over x_lo, z), win: 4 (over y).
Axes of the slice: x: 4 (x_hi: 2, x_lo: 2; x = x_hi * 2 + x_lo), y: 4, z: 8, core: 2. Of those that a mesh axis runs over, the one named last changes fastest.
Arguments:
- spectra: bfloat16 [8192, 8, 2, 256], P(('row', 'col', 'win')), may hold values from -110 to 110
- window_flags: bfloat16 [8192, 256], P(('row', 'col', 'win')), may hold values from 0 to 1, as said below
- station_map: int32 [8192], P(('row', 'col', 'win')), may hold values from 0 to 8191, as said below
Outputs:
- cross_spectra: bfloat16 [8, 2, 8192, 8192], P('win', None, 'row', 'col')
The draws below stay inside these ranges and needn't reach their ends.
Inputs may be any that keep to these rules, and one draw needn't show every extreme that they name: `station_map`: each aligned block of 32 arrival positions holds a permutation of the same block's station numbers. `window_flags`: some stations have weight 0 in every window.
All inputs are finite; a program needn't handle non-finite values.
Results may differ from the reference program's by a relative error of at most 0.0057.
Values may be sent and summed in bfloat16 or wider, within the bound.
A program may use at most 128 MiB of HBM per device.

```python
import jax
import jax.numpy as jnp
from jax import lax

STATIONS = 8192
BINS = 8
WINDOWS = 256
ARRIVE_DEV = 32


def draw_spectra(key, part):
    key = jax.random.fold_in(key, 11)
    subkeys = jax.random.split(key, 5)
    station_gain = jnp.exp(jax.random.uniform(subkeys[0], (STATIONS, 1, 1, 1), minval=-2.3, maxval=2.3))
    window_gain = jnp.exp(jax.random.uniform(subkeys[1], (STATIONS, 1, 1, WINDOWS), minval=-1.0, maxval=1.0))
    recorded = (jax.random.randint(subkeys[4], (STATIONS, 1, 1, WINDOWS), 0, 5) > 0).astype(jnp.float32)
    entries = jnp.clip(jax.random.normal(subkeys[2], (STATIONS, BINS, 2, WINDOWS), jnp.float32), -4.0, 4.0)
    return (entries * station_gain * window_gain * recorded).astype(jnp.bfloat16)


def draw_window_flags(key, part):
    key = jax.random.fold_in(key, 23)
    subkeys = jax.random.split(key, 3)
    working = (jax.random.randint(subkeys[0], (STATIONS, 1), 0, 16) > 0).astype(jnp.float32)
    recorded = (jax.random.randint(subkeys[1], (STATIONS, WINDOWS), 0, 5) < 2).astype(jnp.float32)
    weights = jnp.exp(jax.random.uniform(subkeys[2], (STATIONS, WINDOWS), minval=-3.0, maxval=0.0))
    return (weights * working * recorded).astype(jnp.bfloat16)


def draw_station_map(key, part):
    key = jax.random.fold_in(key, 37)
    block_count = STATIONS // ARRIVE_DEV
    subkeys = jax.random.split(key, block_count)

    def shuffle_block(subkey):
        return jax.random.permutation(subkey, ARRIVE_DEV)
    shuffled = jax.vmap(shuffle_block)(subkeys)
    offsets = ARRIVE_DEV * jnp.arange(block_count)[:, None]
    return (shuffled + offsets).reshape(STATIONS).astype(jnp.int32)


def setup_inputs(seed: int = 0) -> dict:
    streams_of = jax.random.split(jax.random.key(seed), 4)
    spectra = draw_spectra(jax.random.fold_in(streams_of[3], 71), 0)
    window_flags = draw_window_flags(jax.random.fold_in(streams_of[3], 71), 0)
    station_map = draw_station_map(jax.random.fold_in(streams_of[3], 71), 0)
    return {"spectra": spectra, "window_flags": window_flags, "station_map": station_map}


water_level = 0.05

def reference(spectra, window_flags, station_map):
    amplitudes = spectra.astype(jnp.float32)
    band_power = amplitudes[:, :, 0, :] ** 2 + amplitudes[:, :, 1, :] ** 2
    mean_power = lax.optimization_barrier(jnp.mean(band_power, axis=1, keepdims=True))
    window_mask = window_flags.astype(jnp.float32)[:, None, :]
    whitening = lax.rsqrt(band_power + mean_power + water_level) * window_mask
    whitened = (amplitudes * whitening[:, :, None, :]).astype(jnp.bfloat16)
    ordered = jnp.zeros_like(whitened).at[station_map].set(whitened)
    station_flags = jnp.zeros((STATIONS, WINDOWS), jnp.float32).at[station_map].set(window_flags.astype(jnp.float32))
    counts = jnp.dot(station_flags, station_flags.T, precision=lax.Precision.HIGHEST)
    scaling = lax.rsqrt(jnp.maximum(counts, 1.0))
    ordered_data = ordered.astype(jnp.float32)

    def one_bin(freq_bin):
        block_data = lax.dynamic_index_in_dim(ordered_data, freq_bin, 1, keepdims=False)
        real_part = block_data[:, 0, :]
        imag_part = block_data[:, 1, :]
        stack_real = jnp.dot(real_part, real_part.T, precision=lax.Precision.HIGHEST) + jnp.dot(imag_part, imag_part.T, precision=lax.Precision.HIGHEST)
        stack_imag = jnp.dot(imag_part, real_part.T, precision=lax.Precision.HIGHEST) - jnp.dot(real_part, imag_part.T, precision=lax.Precision.HIGHEST)
        return (jnp.stack([stack_real, stack_imag]) * scaling[None]).astype(jnp.bfloat16)
    return lax.map(one_bin, jnp.arange(BINS).astype(jnp.int32))
```

```python
import jax
import jax.numpy as jnp
from jax import lax
from jax.experimental import pallas as pl
from jax.experimental.pallas import tpu as pltpu
from jax.sharding import PartitionSpec as P

MESH = pl.DeviceIdType.MESH
WATER_LEVEL = 0.05


def gather_kernel(
    spec_ref, flag_ref, map_ref, rows, cols, row_flags, col_flags,
    staged, ex_send, ex_recv, z_send, z_recv, x_send, x_recv,
    f_send, f_recv, fx_send, fx_recv, fy_send, fy_recv,
    c_send, c_recv, c_copy, d_send, fc_send, fc_recv, fc_copy, fd_send,
):
    r = lax.axis_index("row")
    c = lax.axis_index("col")
    y = lax.axis_index("win")
    x_hi, core = r // 2, r % 2
    x_lo, z = c // 8, c % 8
    x = x_hi * 2 + x_lo
    other_lo = 1 - x_lo

    def device(xx, cc, zz, yy):
        return {"row": (xx // 2) * 2 + cc, "col": (xx % 2) * 8 + zz, "win": yy}

    z_ids = (device(x, core, (z + 1) % 8, y), device(x, core, (z + 7) % 8, y))
    y_ids = tuple(device(x, core, z, (y + d) % 4) for d in (1, 3, 2))
    x_id = device(x_hi * 2 + other_lo, core, z, y)
    cross_id = device(3 - x, core, z, y)
    twin_id = device(x, 1 - core, z, y)

    barrier = pltpu.get_barrier_semaphore()
    for target in (*z_ids, *y_ids, x_id, cross_id, twin_id):
        pl.semaphore_signal(barrier, inc=1, device_id=target, device_id_type=MESH)

    arrival = lax.broadcasted_iota(jnp.int32, (32, 32), 0)
    onehot = jnp.where(arrival == (map_ref[...] % 32), 1.0, 0.0).astype(jnp.bfloat16)
    flags = flag_ref[...]
    ordered_flags = jnp.dot(onehot, flags, preferred_element_type=jnp.float32)
    row_flags[c, y] = ordered_flags.astype(jnp.bfloat16)
    mask = flags.astype(jnp.float32)
    total = jnp.zeros((32, 256), jnp.float32)
    for f in range(8):
        re = spec_ref[:, f * 512:f * 512 + 256].astype(jnp.float32)
        im = spec_ref[:, f * 512 + 256:f * 512 + 512].astype(jnp.float32)
        total += re * re + im * im
    mean = total * 0.125
    for f in range(8):
        re = spec_ref[:, f * 512:f * 512 + 256].astype(jnp.float32)
        im = spec_ref[:, f * 512 + 256:f * 512 + 512].astype(jnp.float32)
        gain = lax.rsqrt(re * re + im * im + mean + WATER_LEVEL) * mask
        white = jnp.concatenate([re * gain, im * gain], axis=1).astype(jnp.bfloat16)
        staged[f // 2, f % 2] = jnp.dot(
            onehot, white, preferred_element_type=jnp.float32
        ).astype(jnp.bfloat16)
    for b in range(2):
        rows[b, c, pl.ds(y * 32, 32), :] = staged[y, b]

    pl.semaphore_wait(barrier, 8)

    started = []

    def remote(src, dst, send, recv, target):
        copy = pltpu.make_async_remote_copy(
            src_ref=src, dst_ref=dst, send_sem=send, recv_sem=recv,
            device_id=target, device_id_type=MESH,
        )
        copy.start()
        started.append(copy)

    def await_recv(dst, recv):
        pltpu.make_async_remote_copy(
            src_ref=dst, dst_ref=dst, send_sem=recv, recv_sem=recv,
            device_id=twin_id, device_id_type=MESH,
        ).wait_recv()

    def flag_at(s, k):
        return row_flags.at[x_lo * 8 + (z + (8 - k if s == 0 else k)) % 8, y]

    def flag_go(s, k):
        remote(flag_at(s, k), flag_at(s, k), f_send.at[s, k], f_recv.at[s, k], z_ids[s])

    def flag_wait(s, k):
        await_recv(flag_at(s, k), f_recv.at[s, k - 1])

    flag_go(0, 0)
    flag_go(1, 0)

    for b in range(2):
        for i, d in enumerate((1, 3, 2)):
            remote(
                staged.at[(y + d) % 4, b], rows.at[b, c, pl.ds(y * 32, 32)],
                ex_send.at[b, i], ex_recv.at[b, i], y_ids[i],
            )
    for k in (1, 2):
        for s in range(2):
            flag_wait(s, k)
            flag_go(s, k)

    flow_bin = (0, 1, 1)

    def piece_col(flow, s, k):
        lane = other_lo if flow == 2 else x_lo
        return lane * 8 + (z + (8 - k if s == 0 else k)) % 8

    def piece(flow, s, k, half):
        ref = rows.at[flow_bin[flow], piece_col(flow, s, k)]
        return ref.at[pl.ds(64 * s, 64)] if half else ref

    def z_go(flow, k):
        for s in range(2):
            ref = piece(flow, s, k, k == 3)
            remote(ref, ref, z_send.at[flow, s, k], z_recv.at[flow, s, k], z_ids[s])

    def z_wait(flow, k):
        for s in range(2):
            await_recv(piece(flow, s, k, k == 4), z_recv.at[flow, s, k - 1])

    def x_go(slot, ref):
        remote(ref, ref, x_send.at[slot], x_recv.at[slot], x_id)

    def x_ref(lane, slot):
        if slot == 0:
            return rows.at[1, lane * 8 + z]
        if slot == 1:
            return rows.at[0, lane * 8 + z]
        k, s = slot // 2, slot % 2
        ref = rows.at[0, lane * 8 + (z + (8 - k if s == 0 else k)) % 8]
        return ref.at[pl.ds(64 * s, 64)] if k == 4 else ref

    def x_send_slot(slot):
        x_go(slot, x_ref(x_lo, slot))

    def x_wait_slot(slot):
        await_recv(x_ref(other_lo, slot), x_recv.at[slot])

    primary = core == z // 4
    inner = (x == 0) | (x == 3)
    want_lane = (z % 4) // 2
    want_half = z % 2
    hand_x = jnp.where(inner, x, 3 - x)
    hand_core = jnp.where(inner, 1 - core, core)
    hand_id = device(hand_x, hand_core, z, y)

    def hand_copy(b, zz, lane):
        j = zz % 4
        return pltpu.make_async_remote_copy(
            src_ref=rows.at[b, lane * 8 + zz], dst_ref=cols.at[b, j],
            send_sem=c_send.at[b, j], recv_sem=c_recv.at[b, j],
            device_id=hand_id, device_id_type=MESH,
        )

    def local_copy(b, zz, lane):
        j = zz % 4
        return pltpu.make_async_copy(rows.at[b, lane * 8 + zz], cols.at[b, j], c_copy.at[b, j])

    def hand(b, lane, zz):
        @pl.when(primary & (lane == want_lane) & (zz // 4 == want_half))
        def _():
            hand_copy(b, zz, lane).start()

            @pl.when(inner)
            def _():
                local_copy(b, zz, lane).start()

    def hand_flow(flow, k):
        lane = other_lo if flow == 2 else x_lo
        for s in range(1 if k in (0, 4) else 2):
            hand(flow_bin[flow], lane, (z + (8 - k if s == 0 else k)) % 8)

    for i, d in enumerate((1, 3, 2)):
        await_recv(rows.at[0, c, pl.ds(((y + 4 - d) % 4) * 32, 32)], ex_recv.at[0, i])
    z_go(0, 0)
    for i, d in enumerate((1, 3, 2)):
        await_recv(rows.at[1, c, pl.ds(((y + 4 - d) % 4) * 32, 32)], ex_recv.at[1, i])
    x_send_slot(0)
    z_go(1, 0)
    x_send_slot(1)
    hand_flow(0, 0)
    hand_flow(1, 0)

    for s in range(2):
        flag_wait(s, 3)
    flag_go(0, 3)
    flag_wait(0, 4)
    lane_flags = row_flags.at[pl.ds(x_lo * 8, 8), y]
    remote(lane_flags, lane_flags, fx_send.at[0], fx_recv.at[0], x_id)
    for i in range(3):
        remote(lane_flags, lane_flags, fy_send.at[0, i], fy_recv.at[0, i], y_ids[i])

    def step(flow, k):
        z_wait(flow, k)
        if k < 4:
            z_go(flow, k)
        if flow == 0:
            if k < 4:
                x_send_slot(2 * k)
                x_send_slot(2 * k + 1)
            else:
                x_send_slot(8)
                x_send_slot(9)
        hand_flow(flow, k)

    def x_step(k):
        if k == 0:
            x_wait_slot(1)
        else:
            x_wait_slot(2 * k)
            x_wait_slot(2 * k + 1)
        for s in range(1 if k in (0, 4) else 2):
            hand(0, other_lo, (z + (8 - k if s == 0 else k)) % 8)

    step(0, 1)
    x_wait_slot(0)
    z_go(2, 0)
    hand_flow(2, 0)
    far_flags = row_flags.at[pl.ds(other_lo * 8, 8), y]
    await_recv(far_flags, fx_recv.at[0])
    for i in range(3):
        remote(far_flags, far_flags, fy_send.at[1, i], fy_recv.at[1, i], y_ids[i])
    step(0, 2)
    step(1, 1)
    x_step(0)
    step(0, 3)
    step(2, 1)
    x_step(1)
    step(1, 2)
    step(0, 4)
    x_step(2)
    for lane in range(2):
        for i, d in enumerate((1, 3, 2)):
            base = x_lo * 8 if lane == 0 else other_lo * 8
            await_recv(row_flags.at[pl.ds(base, 8), (y + 4 - d) % 4], fy_recv.at[lane, i])

    flag_src = row_flags.at[pl.ds((z % 4) * 4, 4)]
    flag_hand = pltpu.make_async_remote_copy(
        src_ref=flag_src, dst_ref=col_flags, send_sem=fc_send.at[0], recv_sem=fc_recv.at[0],
        device_id=hand_id, device_id_type=MESH,
    )
    flag_local = pltpu.make_async_copy(flag_src, col_flags, fc_copy.at[0])

    @pl.when(primary)
    def _():
        flag_hand.start()

        @pl.when(inner)
        def _():
            flag_local.start()

    step(2, 2)
    step(1, 3)
    x_step(3)
    step(2, 3)
    x_step(4)
    step(1, 4)
    step(2, 4)

    relay = primary & (x != 0) & (x != 3)
    takes = relay | (core != z // 4)

    def relay_copy(b, j):
        return pltpu.make_async_remote_copy(
            src_ref=cols.at[b, j], dst_ref=cols.at[b, j], send_sem=d_send.at[b, j],
            recv_sem=c_recv.at[b, j], device_id=twin_id, device_id_type=MESH,
        )

    flag_relay = pltpu.make_async_remote_copy(
        src_ref=col_flags, dst_ref=col_flags, send_sem=fd_send.at[0], recv_sem=fc_recv.at[0],
        device_id=twin_id, device_id_type=MESH,
    )

    @pl.when(takes)
    def _():
        await_recv(col_flags, fc_recv.at[0])

        @pl.when(relay)
        def _():
            flag_relay.start()

        for b in range(2):
            for j in range(4):
                await_recv(cols.at[b, j], c_recv.at[b, j])

                @pl.when(relay)
                def _():
                    relay_copy(b, j).start()

    for copy in started:
        copy.wait_send()

    @pl.when(primary)
    def _():
        flag_hand.wait_send()
        for b in range(2):
            for j in range(4):
                hand_copy(b, want_half * 4 + j, want_lane).wait_send()

        @pl.when(inner)
        def _():
            flag_local.wait()
            for b in range(2):
                for j in range(4):
                    local_copy(b, want_half * 4 + j, want_lane).wait()

    @pl.when(relay)
    def _():
        flag_relay.wait_send()
        for b in range(2):
            for j in range(4):
                relay_copy(b, j).wait_send()


def gather(spectra, window_flags, station_map):
    vmem = pl.BlockSpec(memory_space=pltpu.VMEM)
    dma = pltpu.SemaphoreType.DMA
    return pl.pallas_call(
        gather_kernel,
        out_shape=(
            jax.ShapeDtypeStruct((2, 16, 128, 512), jnp.bfloat16),
            jax.ShapeDtypeStruct((2, 4, 128, 512), jnp.bfloat16),
            jax.ShapeDtypeStruct((16, 4, 32, 256), jnp.bfloat16),
            jax.ShapeDtypeStruct((4, 4, 32, 256), jnp.bfloat16),
        ),
        in_specs=[vmem] * 3,
        out_specs=(vmem,) * 4,
        scratch_shapes=[
            pltpu.VMEM((4, 2, 32, 512), jnp.bfloat16),
            dma((2, 3)), dma((2, 3)),
            dma((3, 2, 4)), dma((3, 2, 4)),
            dma((10,)), dma((10,)),
            dma((2, 4)), dma((2, 4)),
            dma((1,)), dma((1,)),
            dma((2, 3)), dma((2, 3)),
            dma((2, 4)), dma((2, 4)), dma((2, 4)), dma((2, 4)),
            dma((1,)), dma((1,)), dma((1,)), dma((1,)),
        ],
        compiler_params=pltpu.CompilerParams(
            collective_id=0, has_side_effects=True, vmem_limit_bytes=24 << 20
        ),
        name="gather_rows",
    )(spectra, window_flags, station_map)


def pair_kernel(rows_ref, cols_ref, row_flags_ref, col_flags_ref, out_ref, sides):
    @pl.when(pl.program_id(0) == 0)
    def _():
        for b in range(2):
            both = cols_ref[b].reshape(512, 512)
            sides[b, :512, :] = both
            sides[b, 512:, :256] = -both[:, 256:]
            sides[b, 512:, 256:] = both[:, :256]

    contract = (((1,), (1,)), ((), ()))
    counts = lax.dot_general(
        row_flags_ref[...].reshape(256, 256), col_flags_ref[...].reshape(512, 256),
        contract, preferred_element_type=jnp.float32,
    )
    scaling = lax.rsqrt(jnp.maximum(counts, 1.0))
    for b in range(2):
        block = rows_ref[b].reshape(256, 512)
        for p in range(2):
            tile = lax.dot_general(
                block, sides[b, p * 512:(p + 1) * 512, :], contract,
                preferred_element_type=jnp.float32,
            )
            out_ref[b, p] = (tile * scaling).astype(jnp.bfloat16)


def pairs(rows, cols, row_flags, col_flags):
    return pl.pallas_call(
        pair_kernel,
        grid=(8,),
        out_shape=jax.ShapeDtypeStruct((2, 2, 2048, 512), jnp.bfloat16),
        in_specs=[
            pl.BlockSpec((2, 2, 128, 512), lambda i: (0, i, 0, 0)),
            pl.BlockSpec((2, 4, 128, 512), lambda i: (0, 0, 0, 0)),
            pl.BlockSpec((2, 4, 32, 256), lambda i: (i, 0, 0, 0)),
            pl.BlockSpec((4, 4, 32, 256), lambda i: (0, 0, 0, 0)),
        ],
        out_specs=pl.BlockSpec((2, 2, 256, 512), lambda i: (0, 0, i, 0)),
        scratch_shapes=[pltpu.VMEM((2, 1024, 512), jnp.bfloat16)],
        compiler_params=pltpu.CompilerParams(vmem_limit_bytes=24 << 20),
        name="pair_tiles",
    )(rows, cols, row_flags, col_flags)


def shards(spectra, window_flags, station_map):
    flat = spectra.reshape(32, 4096)
    gathered = gather(flat, window_flags, station_map.reshape(1, 32))
    return pairs(*gathered)


def solution(mesh):
    return jax.shard_map(
        shards,
        mesh=mesh,
        in_specs=(
            P(("row", "col", "win"), None, None, None),
            P(("row", "col", "win"), None),
            P(("row", "col", "win")),
        ),
        out_specs=P("win", None, "row", "col"),
        check_vma=False,
    )
```

```python
import jax
import jax.numpy as jnp
from jax import lax
from jax.experimental import pallas as pl
from jax.experimental.pallas import tpu as pltpu
from jax.sharding import PartitionSpec as P

MESH = pl.DeviceIdType.MESH
WATER_LEVEL = 0.05
NT = (((1,), (1,)), ((), ()))
ORDER = (
    "F1", "O0", "F2", "O1", "A1a", "F3", "A1b", "P0", "FX", "B1", "X0", "A2",
    "FY", "P1", "X1", "R0", "S0", "B2", "A3", "X2", "R1", "S1", "P2", "FH",
    "X3", "R2", "B3", "A4", "FR", "S2", "P3", "W0", "X4", "R3", "B4", "P4",
    "S3", "R4", "E0", "T0", "M01", "S4", "M14", "E1",
)


def turn_columns(cols_ref, b, sides):
    both = cols_ref[b].reshape(512, 512)
    sides[:512, :] = both
    sides[512:, :256] = -both[:, 256:]
    sides[512:, 256:] = both[:, :256]


def pair_part(rows_ref, b, sides, scaling, n):
    tile = lax.dot_general(
        rows_ref[b].reshape(2048, 512), sides[pl.ds(pl.multiple_of(n * 256, 256), 256), :], NT,
        preferred_element_type=jnp.float32,
    )
    return (tile * scaling[:, part_of(n)]).astype(jnp.bfloat16)


def part_of(n):
    return pl.ds(pl.multiple_of((n % 2) * 256, 256), 256)


def gather_kernel(
    spec_ref, flag_ref, map_ref, rows, cols, scaling, first,
    row_flags, col_flags, staged, sides, flag_in, map_in, in_sem,
    ex_send, ex_recv, z_send, z_recv, x_send, x_recv,
    f_send, f_recv, fx_send, fx_recv, fy_send, fy_recv,
    c_send, c_recv, c_copy, d_send, fc_send, fc_recv, fc_copy, fd_send,
):
    flag_copy = pltpu.make_async_copy(flag_ref, flag_in, in_sem.at[0])
    map_copy = pltpu.make_async_copy(map_ref, map_in, in_sem.at[1])
    map_copy.start()
    flag_copy.start()
    r = lax.axis_index("row")
    c = lax.axis_index("col")
    y = lax.axis_index("win")
    x_hi, core = r // 2, r % 2
    x_lo, z = c // 8, c % 8
    x = x_hi * 2 + x_lo
    other_lo = 1 - x_lo

    def device(xx, cc, zz, yy):
        return {"row": (xx // 2) * 2 + cc, "col": (xx % 2) * 8 + zz, "win": yy}

    z_ids = (device(x, core, (z + 1) % 8, y), device(x, core, (z + 7) % 8, y))
    y_at = ((y // 2) * 2 + 1 - y % 2, (y + 2) % 4, 3 - y)
    y_ids = tuple(device(x, core, z, yy) for yy in y_at)
    x_id = device(x_hi * 2 + other_lo, core, z, y)
    cross_id = device(3 - x, core, z, y)
    twin_id = device(x, 1 - core, z, y)

    barrier = pltpu.get_barrier_semaphore()
    for target in (*z_ids, *y_ids, x_id, cross_id, twin_id):
        pl.semaphore_signal(barrier, inc=1, device_id=target, device_id_type=MESH)

    total = jnp.zeros((32, 256), jnp.float32)
    for f in range(8):
        re = spec_ref[:, f * 512:f * 512 + 256].astype(jnp.float32)
        im = spec_ref[:, f * 512 + 256:f * 512 + 512].astype(jnp.float32)
        total += re * re + im * im
    mean = total * 0.125
    map_copy.wait()
    flag_copy.wait()
    arrival = lax.broadcasted_iota(jnp.int32, (32, 32), 0)
    onehot = jnp.where(arrival == (map_in[...] % 32), 1.0, 0.0).astype(jnp.bfloat16)
    flags = flag_in[...]
    ordered_flags = jnp.dot(onehot, flags, preferred_element_type=jnp.float32)
    row_flags[c, y] = ordered_flags.astype(jnp.bfloat16)
    mask = flags.astype(jnp.float32)
    for f in range(8):
        re = spec_ref[:, f * 512:f * 512 + 256].astype(jnp.float32)
        im = spec_ref[:, f * 512 + 256:f * 512 + 512].astype(jnp.float32)
        gain = lax.rsqrt(re * re + im * im + mean + WATER_LEVEL) * mask
        white = jnp.concatenate([re * gain, im * gain], axis=1).astype(jnp.bfloat16)
        staged[f // 2, f % 2] = jnp.dot(
            onehot, white, preferred_element_type=jnp.float32
        ).astype(jnp.bfloat16)
    for b in range(2):
        rows[b, c, pl.ds(y * 32, 32), :] = staged[y, b]

    pl.semaphore_wait(barrier, 8)

    started = []

    def remote(src, dst, send, recv, target):
        copy = pltpu.make_async_remote_copy(
            src_ref=src, dst_ref=dst, send_sem=send, recv_sem=recv,
            device_id=target, device_id_type=MESH,
        )
        copy.start()
        started.append(copy)

    def await_recv(dst, recv):
        pltpu.make_async_remote_copy(
            src_ref=dst, dst_ref=dst, send_sem=recv, recv_sem=recv,
            device_id=twin_id, device_id_type=MESH,
        ).wait_recv()

    def z_from(s, k):
        return (z + (8 - k if s == 0 else k)) % 8

    def flag_at(s, k):
        return row_flags.at[x_lo * 8 + z_from(s, k), y]

    def flag_go(s, k):
        remote(flag_at(s, k), flag_at(s, k), f_send.at[s, k], f_recv.at[s, k], z_ids[s])

    def flag_wait(s, k):
        await_recv(flag_at(s, k), f_recv.at[s, k - 1])

    def exchange(b, i):
        remote(
            staged.at[y_at[i], b], rows.at[b, c, pl.ds(y * 32, 32)],
            ex_send.at[b, i], ex_recv.at[b, i], y_ids[i],
        )

    def exchange_wait(b, i):
        await_recv(rows.at[b, c, pl.ds(y_at[i] * 32, 32)], ex_recv.at[b, i])

    exchange(0, 0)
    exchange(1, 0)
    flag_go(0, 0)
    flag_go(1, 0)
    for b in range(2):
        exchange(b, 1)
        exchange(b, 2)

    kind_bin = (0, 1, 1)

    def half_start(q):
        return (y // 2 if q == 0 else 1 - y // 2) * 64

    def half_of(b, lane, zz, q):
        return rows.at[b, lane * 8 + zz, pl.ds(half_start(q), 64)]

    def lane_of(kind):
        return other_lo if kind == 2 else x_lo

    def sides_of(k, q):
        return (0, 1) if k < 4 else (q,)

    def z_ref(kind, s, k, q):
        return half_of(kind_bin[kind], lane_of(kind), z_from(s, k), q)

    def z_go(kind, s, k, q):
        if k < 3 or s == q:
            ref = z_ref(kind, s, k, q)
            remote(ref, ref, z_send.at[kind, s, k, q], z_recv.at[kind, s, k, q], z_ids[s])

    def z_go_both(kind, q):
        for s in range(2):
            z_go(kind, s, 0, q)

    def z_step(kind, k, q):
        for s in sides_of(k, q):
            await_recv(z_ref(kind, s, k, q), z_recv.at[kind, s, k - 1, q])
            if k < 4:
                z_go(kind, s, k, q)

    def x_slots(k):
        return ((1, 0),) if k == 0 else ((2 * k, 0), (2 * k + 1, 1)) if k < 4 else ((8, 0),)

    def x_go(b, slot, zz, q):
        ref = half_of(b, x_lo, zz, q)
        remote(ref, ref, x_send.at[slot, q], x_recv.at[slot, q], x_id)

    def x_wait(b, slot, zz, q):
        await_recv(half_of(b, other_lo, zz, q), x_recv.at[slot, q])

    primary = core == z // 4
    inner = (x == 0) | (x == 3)
    want_lane = (z % 4) // 2
    want_half = z % 2
    hand_id = device(jnp.where(inner, x, 3 - x), jnp.where(inner, 1 - core, core), z, y)

    def col_half(b, j, q):
        return cols.at[b, j, pl.ds(half_start(q), 64)]

    def hand_copy(b, lane, zz, q):
        j = zz % 4
        return pltpu.make_async_remote_copy(
            src_ref=half_of(b, lane, zz, q), dst_ref=col_half(b, j, q),
            send_sem=c_send.at[b, j, q], recv_sem=c_recv.at[b, j, q],
            device_id=hand_id, device_id_type=MESH,
        )

    def local_copy(b, lane, zz, q):
        j = zz % 4
        return pltpu.make_async_copy(half_of(b, lane, zz, q), col_half(b, j, q), c_copy.at[b, j, q])

    def hand(b, lane, k, q):
        for s in range(1 if k in (0, 4) else 2):
            zz = z_from(s, k)

            @pl.when(primary & (lane == want_lane) & (zz // 4 == want_half))
            def _():
                hand_copy(b, lane, zz, q).start()

                @pl.when(inner)
                def _():
                    local_copy(b, lane, zz, q).start()

    relay = primary & (x != 0) & (x != 3)
    secondary = core != z // 4

    def relay_copy(b, j, q):
        return pltpu.make_async_remote_copy(
            src_ref=col_half(b, j, q), dst_ref=col_half(b, j, q), send_sem=d_send.at[b, j, q],
            recv_sem=c_recv.at[b, j, q], device_id=twin_id, device_id_type=MESH,
        )

    def pass_on(b, k):
        for q in range(2):
            for s in range(1 if k in (0, 4) else 2):
                zz = z_from(s, k)

                @pl.when(relay & (zz // 4 == want_half))
                def _():
                    await_recv(col_half(b, zz % 4, q), c_recv.at[b, zz % 4, q])
                    relay_copy(b, zz % 4, q).start()

    def step(kind, k, q):
        z_step(kind, k, q)
        if kind == 0:
            for slot, s in x_slots(k):
                x_go(0, slot, z_from(s, k), q)
        hand(kind_bin[kind], lane_of(kind), k, q)

    def x_step(k):
        for q in range(2):
            for slot, s in x_slots(k):
                x_wait(0, slot, z_from(s, k), q)
            hand(0, other_lo, k, q)

    def both(kind, k):
        for q in range(2):
            step(kind, k, q)

    def open_half(q):
        for b in range(2):
            for i in (0,) if q == 0 else (1, 2):
                exchange_wait(b, i)
            z_go_both(b, q)
        x_go(1, 0, z, q)
        x_go(0, 1, z, q)
        hand(0, x_lo, 0, q)
        hand(1, x_lo, 0, q)

    def open_other(q):
        x_wait(1, 0, z, q)
        z_go_both(2, q)
        hand(1, other_lo, 0, q)

    def flag_step(k):
        for s in range(2):
            flag_wait(s, k)
            if k < 3:
                flag_go(s, k)
        if k == 3:
            flag_go(0, 3)

    def flags_x():
        flag_wait(0, 4)
        lane_flags = row_flags.at[pl.ds(x_lo * 8, 8), y]
        remote(lane_flags, lane_flags, fx_send.at[0], fx_recv.at[0], x_id)
        for i in range(3):
            remote(lane_flags, lane_flags, fy_send.at[0, i], fy_recv.at[0, i], y_ids[i])

    def flags_y():
        far_flags = row_flags.at[pl.ds(other_lo * 8, 8), y]
        await_recv(far_flags, fx_recv.at[0])
        for i in range(3):
            remote(far_flags, far_flags, fy_send.at[1, i], fy_recv.at[1, i], y_ids[i])

    flag_src = row_flags.at[pl.ds((z % 4) * 4, 4)]
    flag_hand = pltpu.make_async_remote_copy(
        src_ref=flag_src, dst_ref=col_flags, send_sem=fc_send.at[0], recv_sem=fc_recv.at[0],
        device_id=hand_id, device_id_type=MESH,
    )
    flag_local = pltpu.make_async_copy(flag_src, col_flags, fc_copy.at[0])
    flag_relay = pltpu.make_async_remote_copy(
        src_ref=col_flags, dst_ref=col_flags, send_sem=fd_send.at[0], recv_sem=fc_recv.at[0],
        device_id=twin_id, device_id_type=MESH,
    )

    def flags_hand():
        for lane in range(2):
            for i in range(3):
                base = x_lo * 8 if lane == 0 else other_lo * 8
                await_recv(row_flags.at[pl.ds(base, 8), y_at[i]], fy_recv.at[lane, i])

        @pl.when(primary)
        def _():
            flag_hand.start()

            @pl.when(inner)
            def _():
                flag_local.start()

    def flags_pass():
        @pl.when(relay)
        def _():
            await_recv(col_flags, fc_recv.at[0])
            flag_relay.start()

    def settle(b):
        @pl.when(secondary)
        def _():
            for j in range(4):
                for q in range(2):
                    await_recv(col_half(b, j, q), c_recv.at[b, j, q])

        @pl.when(primary & inner)
        def _():
            for j in range(4):
                for q in range(2):
                    local_copy(b, want_lane, want_half * 4 + j, q).wait()

    def weights():
        @pl.when(secondary)
        def _():
            await_recv(col_flags, fc_recv.at[0])

        @pl.when(primary & inner)
        def _():
            flag_local.wait()

        for half in range(2):
            counts = lax.dot_general(
                row_flags[...].reshape(2048, 256), col_flags[2 * half:2 * half + 2].reshape(256, 256), NT,
                preferred_element_type=jnp.float32,
            )
            scaling[:, half * 256:(half + 1) * 256] = lax.rsqrt(jnp.maximum(counts, 1.0))

    def tile(n):
        first[n // 2, :, part_of(n)] = pair_part(rows, 0, sides, scaling, n)

    flag_steps = {
        "F1": lambda: flag_step(1), "F2": lambda: flag_step(2), "F3": lambda: flag_step(3),
        "FX": flags_x, "FY": flags_y, "FH": flags_hand, "FR": flags_pass, "W0": weights,
    }
    for token in ORDER:
        kind, k = token[0], token[1]
        if kind in "FW":
            flag_steps[token]()
        elif kind == "E":
            settle(int(k))
        elif kind == "T":
            turn_columns(cols, 0, sides)
        elif kind == "M":
            pl.loop(int(k), int(token[2]))(tile)
        elif kind == "O":
            open_half(int(k))
        elif kind == "X":
            x_step(int(k))
        elif kind in "RS":
            pass_on("RS".index(kind), int(k))
        else:
            for q in ("ab".index(token[2]),) if len(token) > 2 else (0, 1):
                if kind == "P" and k == "0":
                    open_other(q)
                else:
                    step("ABP".index(kind), int(k), q)

    for copy in started:
        copy.wait_send()

    @pl.when(primary)
    def _():
        flag_hand.wait_send()
        for b in range(2):
            for j in range(4):
                for q in range(2):
                    hand_copy(b, want_lane, want_half * 4 + j, q).wait_send()

    @pl.when(relay)
    def _():
        flag_relay.wait_send()
        for b in range(2):
            for j in range(4):
                for q in range(2):
                    relay_copy(b, j, q).wait_send()


def gather(spectra, window_flags, station_map):
    vmem = pl.BlockSpec(memory_space=pltpu.VMEM)
    hbm = pl.BlockSpec(memory_space=pltpu.HBM)
    dma = pltpu.SemaphoreType.DMA
    return pl.pallas_call(
        gather_kernel,
        out_shape=(
            jax.ShapeDtypeStruct((2, 16, 128, 512), jnp.bfloat16),
            jax.ShapeDtypeStruct((2, 4, 128, 512), jnp.bfloat16),
            jax.ShapeDtypeStruct((2048, 512), jnp.float32),
            jax.ShapeDtypeStruct((2, 2048, 512), jnp.bfloat16),
        ),
        in_specs=[vmem, hbm, hbm],
        out_specs=(vmem,) * 4,
        scratch_shapes=[
            pltpu.VMEM((16, 4, 32, 256), jnp.bfloat16),
            pltpu.VMEM((4, 4, 32, 256), jnp.bfloat16),
            pltpu.VMEM((4, 2, 32, 512), jnp.bfloat16),
            pltpu.VMEM((1024, 512), jnp.bfloat16),
            pltpu.VMEM((32, 256), jnp.bfloat16),
            pltpu.VMEM((1, 32), jnp.int32),
            dma((2,)),
            dma((2, 3)), dma((2, 3)),
            dma((3, 2, 4, 2)), dma((3, 2, 4, 2)),
            dma((9, 2)), dma((9, 2)),
            dma((2, 4)), dma((2, 4)),
            dma((1,)), dma((1,)),
            dma((2, 3)), dma((2, 3)),
            dma((2, 4, 2)), dma((2, 4, 2)), dma((2, 4, 2)), dma((2, 4, 2)),
            dma((1,)), dma((1,)), dma((1,)), dma((1,)),
        ],
        compiler_params=pltpu.CompilerParams(
            collective_id=0, has_side_effects=True, vmem_limit_bytes=32 << 20
        ),
        name="gather_rows",
    )(spectra, window_flags, station_map)


def finish_kernel(rows, cols, scaling, first, out, sides, second, sems):
    done = pltpu.make_async_copy(first, out.at[0], sems.at[0])
    done.start()
    turn_columns(cols, 1, sides)

    def copy_out(n):
        return pltpu.make_async_copy(
            second.at[n // 2, :, part_of(n)], out.at[1, n // 2, :, part_of(n)], sems.at[1 + n]
        )

    @pl.loop(0, 4)
    def _(n):
        second[n // 2, :, part_of(n)] = pair_part(rows, 1, sides, scaling, n)
        copy_out(n).start()

    done.wait()
    for n in range(4):
        copy_out(n).wait()


def finish(rows, cols, scaling, first):
    vmem = pl.BlockSpec(memory_space=pltpu.VMEM)
    return pl.pallas_call(
        finish_kernel,
        out_shape=jax.ShapeDtypeStruct((2, 2, 2048, 512), jnp.bfloat16),
        in_specs=[vmem] * 4,
        out_specs=pl.BlockSpec(memory_space=pltpu.HBM),
        scratch_shapes=[
            pltpu.VMEM((1024, 512), jnp.bfloat16),
            pltpu.VMEM((2, 2048, 512), jnp.bfloat16),
            pltpu.SemaphoreType.DMA((5,)),
        ],
        compiler_params=pltpu.CompilerParams(vmem_limit_bytes=24 << 20),
        name="finish_pairs",
    )(rows, cols, scaling, first)


def run_gather(spectra, window_flags, station_map):
    flat = spectra.reshape(32, 4096)
    return gather(
        flat, pltpu.with_memory_space_constraint(window_flags, pltpu.HBM),
        pltpu.with_memory_space_constraint(station_map.reshape(1, 32), pltpu.HBM),
    )


def shards(spectra, window_flags, station_map):
    return finish(*run_gather(spectra, window_flags, station_map))


def solution(mesh):
    return jax.shard_map(
        shards,
        mesh=mesh,
        in_specs=(
            P(("row", "col", "win"), None, None, None),
            P(("row", "col", "win"), None),
            P(("row", "col", "win")),
        ),
        out_specs=P("win", None, "row", "col"),
        check_vma=False,
    )
```

```python
import jax
import jax.numpy as jnp
from jax import lax
from jax.experimental import pallas as pl
from jax.experimental.pallas import tpu as pltpu
from jax.sharding import PartitionSpec as P

MESH = pl.DeviceIdType.MESH
WATER_LEVEL = 0.05
NT = (((1,), (1,)), ((), ()))
ORDER = (
    "F1", "O0", "F2", "O1", "A1a", "F3", "A1b", "P0", "FX", "B1", "X0", "A2",
    "FY", "P1", "X1", "R0", "S0", "B2", "A3", "X2", "FH", "R1", "S1", "P2",
    "X3", "FR", "R2", "B3", "A4", "S2", "P3", "W0", "X4", "R3", "B4", "P4",
    "S3", "R4", "E0", "T0", "M01", "S4", "M14", "E1",
)


def turn_columns(cols_ref, b, sides):
    both = cols_ref[b].reshape(512, 512)
    sides[:512, :] = both
    sides[512:, :256] = -both[:, 256:]
    sides[512:, 256:] = both[:, :256]


def pair_part(rows_ref, b, sides, scaling, n):
    tile = lax.dot_general(
        rows_ref[b].reshape(2048, 512), sides[pl.ds(pl.multiple_of(n * 256, 256), 256), :], NT,
        preferred_element_type=jnp.float32,
    )
    return (tile * scaling[:, part_of(n)]).astype(jnp.bfloat16)


def part_of(n):
    return pl.ds(pl.multiple_of((n % 2) * 256, 256), 256)


def gather_kernel(
    spec_ref, flag_ref, map_ref, rows, cols, scaling, first,
    row_flags, col_flags, staged, sides, flag_in, map_in, in_sem,
    ex_send, ex_recv, zo_send, zo_recv, xo_send, xo_recv, z_send, z_recv, x_send, x_recv,
    f_send, f_recv, fx_send, fx_recv, fy_send, fy_recv,
    c_send, c_recv, c_copy, d_send, fc_send, fc_recv, fc_copy, fd_send,
):
    flag_copy = pltpu.make_async_copy(flag_ref, flag_in, in_sem.at[0])
    map_copy = pltpu.make_async_copy(map_ref, map_in, in_sem.at[1])
    map_copy.start()
    flag_copy.start()
    r = lax.axis_index("row")
    c = lax.axis_index("col")
    y = lax.axis_index("win")
    x_hi, core = r // 2, r % 2
    x_lo, z = c // 8, c % 8
    x = x_hi * 2 + x_lo
    other_lo = 1 - x_lo

    def device(xx, cc, zz, yy):
        return {"row": (xx // 2) * 2 + cc, "col": (xx % 2) * 8 + zz, "win": yy}

    z_ids = (device(x, core, (z + 1) % 8, y), device(x, core, (z + 7) % 8, y))
    y_at = ((y // 2) * 2 + 1 - y % 2, (y + 2) % 4, 3 - y)
    y_ids = tuple(device(x, core, z, yy) for yy in y_at)
    x_id = device(x_hi * 2 + other_lo, core, z, y)
    cross_id = device(3 - x, core, z, y)
    twin_id = device(x, 1 - core, z, y)

    barrier = pltpu.get_barrier_semaphore()
    for target in (*z_ids, *y_ids, x_id, cross_id, twin_id):
        pl.semaphore_signal(barrier, inc=1, device_id=target, device_id_type=MESH)

    total = jnp.zeros((32, 256), jnp.float32)
    for f in range(8):
        re = spec_ref[:, f * 512:f * 512 + 256].astype(jnp.float32)
        im = spec_ref[:, f * 512 + 256:f * 512 + 512].astype(jnp.float32)
        total += re * re + im * im
    mean = total * 0.125
    map_copy.wait()
    flag_copy.wait()
    arrival = lax.broadcasted_iota(jnp.int32, (32, 32), 0)
    onehot = jnp.where(arrival == (map_in[...] % 32), 1.0, 0.0).astype(jnp.bfloat16)
    flags = flag_in[...]
    ordered_flags = jnp.dot(onehot, flags, preferred_element_type=jnp.float32)
    row_flags[c, y] = ordered_flags.astype(jnp.bfloat16)
    mask = flags.astype(jnp.float32)
    for f in range(8):
        re = spec_ref[:, f * 512:f * 512 + 256].astype(jnp.float32)
        im = spec_ref[:, f * 512 + 256:f * 512 + 512].astype(jnp.float32)
        gain = lax.rsqrt(re * re + im * im + mean + WATER_LEVEL) * mask
        white = jnp.concatenate([re * gain, im * gain], axis=1).astype(jnp.bfloat16)
        staged[f // 2, f % 2] = jnp.dot(
            onehot, white, preferred_element_type=jnp.float32
        ).astype(jnp.bfloat16)
    for b in range(2):
        rows[b, c, pl.ds(y * 32, 32), :] = staged[y, b]

    pl.semaphore_wait(barrier, 8)

    started = []

    def remote(src, dst, send, recv, target):
        copy = pltpu.make_async_remote_copy(
            src_ref=src, dst_ref=dst, send_sem=send, recv_sem=recv,
            device_id=target, device_id_type=MESH,
        )
        copy.start()
        started.append(copy)

    def await_recv(dst, recv):
        pltpu.make_async_remote_copy(
            src_ref=dst, dst_ref=dst, send_sem=recv, recv_sem=recv,
            device_id=twin_id, device_id_type=MESH,
        ).wait_recv()

    def z_from(s, k):
        return (z + (8 - k if s == 0 else k)) % 8

    def flag_at(s, k):
        return row_flags.at[x_lo * 8 + z_from(s, k), y]

    def flag_go(s, k):
        remote(flag_at(s, k), flag_at(s, k), f_send.at[s, k], f_recv.at[s, k], z_ids[s])

    def flag_wait(s, k):
        await_recv(flag_at(s, k), f_recv.at[s, k - 1])

    def exchange(b, i):
        remote(
            staged.at[y_at[i], b], rows.at[b, c, pl.ds(y * 32, 32)],
            ex_send.at[b, i], ex_recv.at[b, i], y_ids[i],
        )

    def exchange_wait(b, i):
        await_recv(rows.at[b, c, pl.ds(y_at[i] * 32, 32)], ex_recv.at[b, i])

    def quarter(b, lane, zz, i):
        return rows.at[b, lane * 8 + zz, pl.ds((y if i == 0 else y_at[0]) * 32, 32)]

    flag_go(0, 0)
    flag_go(1, 0)
    exchange(0, 0)
    exchange(1, 0)
    for b in range(2):
        own = quarter(b, x_lo, z, 0)
        for s in range(2):
            remote(own, own, zo_send.at[b, s], zo_recv.at[b, s], z_ids[s])
        far = quarter(1 - b, x_lo, z, 0)
        remote(far, far, xo_send.at[b], xo_recv.at[b], x_id)
        exchange(b, 1)
        exchange(b, 2)

    kind_bin = (0, 1, 1)

    def half_start(q):
        return (y // 2 if q == 0 else 1 - y // 2) * 64

    def half_of(b, lane, zz, q):
        return rows.at[b, lane * 8 + zz, pl.ds(half_start(q), 64)]

    def lane_of(kind):
        return other_lo if kind == 2 else x_lo

    def sides_of(k, q):
        return (0, 1) if k < 4 else (q,)

    def z_ref(kind, s, k, q):
        return half_of(kind_bin[kind], lane_of(kind), z_from(s, k), q)

    def z_go(kind, s, k, q):
        if k < 3 or s == q:
            opening = kind < 2 and k == 0 and q == 0
            ref = quarter(kind, x_lo, z, 1) if opening else z_ref(kind, s, k, q)
            remote(ref, ref, z_send.at[kind, s, k, q], z_recv.at[kind, s, k, q], z_ids[s])

    def z_go_both(kind, q):
        for s in range(2):
            z_go(kind, s, 0, q)

    def z_step(kind, k, q):
        for s in sides_of(k, q):
            if kind < 2 and k == 1 and q == 0:
                await_recv(quarter(kind, x_lo, z_from(s, 1), 0), zo_recv.at[kind, s])
                await_recv(quarter(kind, x_lo, z_from(s, 1), 1), z_recv.at[kind, s, 0, 0])
            else:
                await_recv(z_ref(kind, s, k, q), z_recv.at[kind, s, k - 1, q])
            if k < 4:
                z_go(kind, s, k, q)

    def x_slots(k):
        return ((1, 0),) if k == 0 else ((2 * k, 0), (2 * k + 1, 1)) if k < 4 else ((8, 0),)

    def x_go(b, slot, zz, q):
        ref = quarter(b, x_lo, z, 1) if slot < 2 and q == 0 else half_of(b, x_lo, zz, q)
        remote(ref, ref, x_send.at[slot, q], x_recv.at[slot, q], x_id)

    def x_wait(b, slot, zz, q):
        if slot < 2 and q == 0:
            await_recv(quarter(b, other_lo, z, 0), xo_recv.at[slot])
            await_recv(quarter(b, other_lo, z, 1), x_recv.at[slot, 0])
        else:
            await_recv(half_of(b, other_lo, zz, q), x_recv.at[slot, q])

    primary = core == z // 4
    inner = (x == 0) | (x == 3)
    want_lane = (z % 4) // 2
    want_half = z % 2
    hand_id = device(jnp.where(inner, x, 3 - x), jnp.where(inner, 1 - core, core), z, y)

    def col_half(b, j, q):
        return cols.at[b, j, pl.ds(half_start(q), 64)]

    def hand_copy(b, lane, zz, q):
        j = zz % 4
        return pltpu.make_async_remote_copy(
            src_ref=half_of(b, lane, zz, q), dst_ref=col_half(b, j, q),
            send_sem=c_send.at[b, j, q], recv_sem=c_recv.at[b, j, q],
            device_id=hand_id, device_id_type=MESH,
        )

    def local_copy(b, lane, zz, q):
        j = zz % 4
        return pltpu.make_async_copy(half_of(b, lane, zz, q), col_half(b, j, q), c_copy.at[b, j, q])

    def hand(b, lane, k, q):
        for s in range(1 if k in (0, 4) else 2):
            zz = z_from(s, k)

            @pl.when(primary & (lane == want_lane) & (zz // 4 == want_half))
            def _():
                hand_copy(b, lane, zz, q).start()

                @pl.when(inner)
                def _():
                    local_copy(b, lane, zz, q).start()

    relay = primary & (x != 0) & (x != 3)
    secondary = core != z // 4

    def relay_copy(b, j, q):
        return pltpu.make_async_remote_copy(
            src_ref=col_half(b, j, q), dst_ref=col_half(b, j, q), send_sem=d_send.at[b, j, q],
            recv_sem=c_recv.at[b, j, q], device_id=twin_id, device_id_type=MESH,
        )

    def pass_on(b, k):
        for q in range(2):
            for s in range(1 if k in (0, 4) else 2):
                zz = z_from(s, k)

                @pl.when(relay & (zz // 4 == want_half))
                def _():
                    await_recv(col_half(b, zz % 4, q), c_recv.at[b, zz % 4, q])
                    relay_copy(b, zz % 4, q).start()

    def step(kind, k, q):
        z_step(kind, k, q)
        if kind == 0:
            for slot, s in x_slots(k):
                x_go(0, slot, z_from(s, k), q)
        hand(kind_bin[kind], lane_of(kind), k, q)

    def x_step(k):
        for q in range(2):
            for slot, s in x_slots(k):
                x_wait(0, slot, z_from(s, k), q)
            hand(0, other_lo, k, q)

    def both(kind, k):
        for q in range(2):
            step(kind, k, q)

    def open_half(q):
        for b in range(2):
            for i in (0,) if q == 0 else (1, 2):
                exchange_wait(b, i)
            z_go_both(b, q)
        x_go(1, 0, z, q)
        x_go(0, 1, z, q)
        hand(0, x_lo, 0, q)
        hand(1, x_lo, 0, q)

    def open_other(q):
        x_wait(1, 0, z, q)
        z_go_both(2, q)
        hand(1, other_lo, 0, q)

    def flag_step(k):
        for s in range(2):
            flag_wait(s, k)
            if k < 3:
                flag_go(s, k)
        if k == 3:
            flag_go(0, 3)

    def flags_x():
        flag_wait(0, 4)
        lane_flags = row_flags.at[pl.ds(x_lo * 8, 8), y]
        remote(lane_flags, lane_flags, fx_send.at[0], fx_recv.at[0], x_id)
        for i in range(3):
            remote(lane_flags, lane_flags, fy_send.at[0, i], fy_recv.at[0, i], y_ids[i])

    def flags_y():
        far_flags = row_flags.at[pl.ds(other_lo * 8, 8), y]
        await_recv(far_flags, fx_recv.at[0])
        for i in range(3):
            remote(far_flags, far_flags, fy_send.at[1, i], fy_recv.at[1, i], y_ids[i])

    flag_src = row_flags.at[pl.ds((z % 4) * 4, 4)]
    flag_hand = pltpu.make_async_remote_copy(
        src_ref=flag_src, dst_ref=col_flags, send_sem=fc_send.at[0], recv_sem=fc_recv.at[0],
        device_id=hand_id, device_id_type=MESH,
    )
    flag_local = pltpu.make_async_copy(flag_src, col_flags, fc_copy.at[0])
    flag_relay = pltpu.make_async_remote_copy(
        src_ref=col_flags, dst_ref=col_flags, send_sem=fd_send.at[0], recv_sem=fc_recv.at[0],
        device_id=twin_id, device_id_type=MESH,
    )

    def flags_hand():
        for lane in range(2):
            for i in range(3):
                base = x_lo * 8 if lane == 0 else other_lo * 8
                await_recv(row_flags.at[pl.ds(base, 8), y_at[i]], fy_recv.at[lane, i])

        @pl.when(primary)
        def _():
            flag_hand.start()

            @pl.when(inner)
            def _():
                flag_local.start()

    def flags_pass():
        @pl.when(relay)
        def _():
            await_recv(col_flags, fc_recv.at[0])
            flag_relay.start()

    def settle(b):
        @pl.when(secondary)
        def _():
            for j in range(4):
                for q in range(2):
                    await_recv(col_half(b, j, q), c_recv.at[b, j, q])

        @pl.when(primary & inner)
        def _():
            for j in range(4):
                for q in range(2):
                    local_copy(b, want_lane, want_half * 4 + j, q).wait()

    def weights():
        @pl.when(secondary)
        def _():
            await_recv(col_flags, fc_recv.at[0])

        @pl.when(primary & inner)
        def _():
            flag_local.wait()

        @pl.loop(0, 2)
        def _(half):
            counts = lax.dot_general(
                row_flags[...].reshape(2048, 256), col_flags[pl.ds(2 * half, 2)].reshape(256, 256), NT,
                preferred_element_type=jnp.float32,
            )
            scaling[:, part_of(half)] = lax.rsqrt(jnp.maximum(counts, 1.0))

    def tile(n):
        first[n // 2, :, part_of(n)] = pair_part(rows, 0, sides, scaling, n)

    flag_steps = {
        "F1": lambda: flag_step(1), "F2": lambda: flag_step(2), "F3": lambda: flag_step(3),
        "FX": flags_x, "FY": flags_y, "FH": flags_hand, "FR": flags_pass, "W0": weights,
    }
    for token in ORDER:
        kind, k = token[0], token[1]
        if kind in "FW":
            flag_steps[token]()
        elif kind == "E":
            settle(int(k))
        elif kind == "T":
            turn_columns(cols, 0, sides)
        elif kind == "M":
            pl.loop(int(k), int(token[2]))(tile)
        elif kind == "O":
            open_half(int(k))
        elif kind == "X":
            x_step(int(k))
        elif kind in "RS":
            pass_on("RS".index(kind), int(k))
        else:
            for q in ("ab".index(token[2]),) if len(token) > 2 else (0, 1):
                if kind == "P" and k == "0":
                    open_other(q)
                else:
                    step("ABP".index(kind), int(k), q)

    for copy in started:
        copy.wait_send()

    @pl.when(primary)
    def _():
        flag_hand.wait_send()
        for b in range(2):
            for j in range(4):
                for q in range(2):
                    hand_copy(b, want_lane, want_half * 4 + j, q).wait_send()

    @pl.when(relay)
    def _():
        flag_relay.wait_send()
        for b in range(2):
            for j in range(4):
                for q in range(2):
                    relay_copy(b, j, q).wait_send()


def gather(spectra, window_flags, station_map):
    vmem = pl.BlockSpec(memory_space=pltpu.VMEM)
    hbm = pl.BlockSpec(memory_space=pltpu.HBM)
    dma = pltpu.SemaphoreType.DMA
    return pl.pallas_call(
        gather_kernel,
        out_shape=(
            jax.ShapeDtypeStruct((2, 16, 128, 512), jnp.bfloat16),
            jax.ShapeDtypeStruct((2, 4, 128, 512), jnp.bfloat16),
            jax.ShapeDtypeStruct((2048, 512), jnp.float32),
            jax.ShapeDtypeStruct((2, 2048, 512), jnp.bfloat16),
        ),
        in_specs=[vmem, hbm, hbm],
        out_specs=(vmem,) * 4,
        scratch_shapes=[
            pltpu.VMEM((16, 4, 32, 256), jnp.bfloat16),
            pltpu.VMEM((4, 4, 32, 256), jnp.bfloat16),
            pltpu.VMEM((4, 2, 32, 512), jnp.bfloat16),
            pltpu.VMEM((1024, 512), jnp.bfloat16),
            pltpu.VMEM((32, 256), jnp.bfloat16),
            pltpu.VMEM((1, 32), jnp.int32),
            dma((2,)),
            dma((2, 3)), dma((2, 3)),
            dma((2, 2)), dma((2, 2)), dma((2,)), dma((2,)),
            dma((3, 2, 4, 2)), dma((3, 2, 4, 2)),
            dma((9, 2)), dma((9, 2)),
            dma((2, 4)), dma((2, 4)),
            dma((1,)), dma((1,)),
            dma((2, 3)), dma((2, 3)),
            dma((2, 4, 2)), dma((2, 4, 2)), dma((2, 4, 2)), dma((2, 4, 2)),
            dma((1,)), dma((1,)), dma((1,)), dma((1,)),
        ],
        compiler_params=pltpu.CompilerParams(
            collective_id=0, has_side_effects=True, vmem_limit_bytes=32 << 20
        ),
        name="gather_rows",
    )(spectra, window_flags, station_map)


def finish_kernel(rows, cols, scaling, first, out, sides, second, sems):
    done = pltpu.make_async_copy(first, out.at[0], sems.at[0])
    done.start()
    turn_columns(cols, 1, sides)

    def copy_out(n):
        return pltpu.make_async_copy(
            second.at[n // 2, :, part_of(n)], out.at[1, n // 2, :, part_of(n)], sems.at[1 + n]
        )

    @pl.loop(0, 4)
    def _(n):
        second[n // 2, :, part_of(n)] = pair_part(rows, 1, sides, scaling, n)
        copy_out(n).start()

    done.wait()
    for n in range(4):
        copy_out(n).wait()


def finish(rows, cols, scaling, first):
    vmem = pl.BlockSpec(memory_space=pltpu.VMEM)
    return pl.pallas_call(
        finish_kernel,
        out_shape=jax.ShapeDtypeStruct((2, 2, 2048, 512), jnp.bfloat16),
        in_specs=[vmem] * 4,
        out_specs=pl.BlockSpec(memory_space=pltpu.HBM),
        scratch_shapes=[
            pltpu.VMEM((1024, 512), jnp.bfloat16),
            pltpu.VMEM((2, 2048, 512), jnp.bfloat16),
            pltpu.SemaphoreType.DMA((5,)),
        ],
        compiler_params=pltpu.CompilerParams(vmem_limit_bytes=24 << 20),
        name="finish_pairs",
    )(rows, cols, scaling, first)


def run_gather(spectra, window_flags, station_map):
    flat = spectra.reshape(32, 4096)
    return gather(
        flat, pltpu.with_memory_space_constraint(window_flags, pltpu.HBM),
        pltpu.with_memory_space_constraint(station_map.reshape(1, 32), pltpu.HBM),
    )


def shards(spectra, window_flags, station_map):
    return finish(*run_gather(spectra, window_flags, station_map))


def solution(mesh):
    return jax.shard_map(
        shards,
        mesh=mesh,
        in_specs=(
            P(("row", "col", "win"), None, None, None),
            P(("row", "col", "win"), None),
            P(("row", "col", "win")),
        ),
        out_specs=P("win", None, "row", "col"),
        check_vma=False,
    )
```
